32 devices in a mesh: dom: 8 (over z, y), sub: 4 (over x, core).
Axes of the slice: x: 2, y: 2, z: 4, core: 2. Of those that a mesh axis runs over, the one named last changes fastest.
Arguments:
- rhs: float32 [6, 16384], P(None, ('dom', 'sub')), may hold values from -6 to 6
- precond: float32 [6, 6, 16384], P(None, None, ('dom', 'sub'))
- diag_blocks: float32 [6, 6, 16384], P(None, None, ('dom', 'sub'))
- off_blocks: float32 [6, 6, 6, 16384], P(None, None, None, ('dom', 'sub')), may hold values from -0.5 to 0.5
- neighbours: int32 [6, 16384], P(None, ('dom', 'sub')), may hold values from 0 to 1023
- colours: int32 [16384], P(('dom', 'sub')), may hold values from 0 to 3, as said below
- send_lists: int32 [4, 4, 1024], P(None, None, ('dom', 'sub')), may hold values from 0 to 511, as said below
Outputs:
- correction: float32 [6, 16384], P(None, ('dom', 'sub'))
- new_residual: float32 [6, 16384], P(None, ('dom', 'sub'))
The draws below stay inside these ranges and needn't reach their ends.
Inputs may be any that keep to these rules, and one draw needn't show every extreme that they name: colours[n] equals c exactly for the nodes listed under colour c in its device's send_lists; each colour holds 128 nodes of every device. `send_lists`: on each device the 512 entries are the 512 local nodes, each once; entry [d, c, h] is a node of colour c.
All inputs are finite; a program needn't handle non-finite values.
Results may differ from the reference program's by a relative error of at most 0.0001.
Values sent between devices are 32-bit elements; how exact they have to be, the bound alone decides.
A program may use at most 64 MiB of HBM per device.

```python
import jax
import jax.numpy as jnp
from jax import lax

VARS = 6
NBRS = 6
NODES_DEV = 512
HALO_SLOTS = 32
DOMAINS = 32
NODES = 16384
N_DOM = 8
N_SUB = 4


def layout(key):
    keys = jax.random.split(key, DOMAINS)
    return jax.vmap(lambda single: jax.random.permutation(single, NODES_DEV))(keys).astype(jnp.int32)


def draw_send_lists(key, part):
    order = layout(key)
    lists = order.reshape(DOMAINS, 4, 4, HALO_SLOTS).transpose(1, 2, 0, 3)
    return lists.reshape(4, 4, DOMAINS * HALO_SLOTS).astype(jnp.int32)


def draw_colours(key, part):
    order = layout(key)
    place = jnp.argsort(order, axis=1, stable=True).astype(jnp.int32)
    shade = place // HALO_SLOTS % 4
    return shade.reshape(NODES).astype(jnp.int32)


def block_draw(key, low, high, spread):
    key_diag, key_off = jax.random.split(key)
    shape = (VARS, VARS, NODES)
    diagonal = jax.random.uniform(key_diag, shape, jnp.float32, low, high)
    offside = jax.random.uniform(key_off, shape, jnp.float32, -spread, spread)
    rows = lax_iota(0)
    cols = lax_iota(1)
    return jnp.where((rows == cols)[:, :, None], diagonal, offside).astype(jnp.float32)


def lax_iota(dim):
    return jax.lax.broadcasted_iota(jnp.int32, (VARS, VARS), dim)


def draw_precond(key, part):
    key = jax.random.fold_in(key, 11)
    return block_draw(key, 0.6, 1.2, 0.15)


def draw_diag_blocks(key, part):
    key = jax.random.fold_in(key, 12)
    return block_draw(key, 1.5, 3.0, 0.3)


def touch_ends(array, own_key, least, high):
    shape = array.shape
    spot = [jax.random.randint(jax.random.fold_in(own_key, axis), (), 0, shape[axis]) for axis in range(len(shape))]
    array = array.at[tuple(spot)].set(least)
    longest = shape.index(max(shape))
    spot[longest] = (spot[longest] + 1) % shape[longest]
    return array.at[tuple(spot)].set(high)


def block_scale(stream_key, dims, cuts, least, high):
    def one(position, blocks):
        steps = jax.random.uniform(jax.random.fold_in(jax.random.fold_in(stream_key, 6), position), (blocks,), jnp.float32, least / len(cuts), high / len(cuts))
        return jnp.repeat(jnp.exp(steps), dims[position] // blocks).reshape((-1,) + (1,) * (len(dims) - position - 1))

    level = one(*cuts[0])
    for cut in cuts[1:]:
        level = level * one(*cut)
    return level


def bell_draw(stream_key, dims, scale, bound, pieces=(), kind=jnp.bfloat16):
    level = block_scale(stream_key, dims, pieces, -0.22, 0.18) if pieces else 1.0
    drawn = jax.random.normal(stream_key, dims, jnp.float32) * scale * level
    return jnp.minimum(jnp.maximum(drawn, -bound), bound).astype(kind)


def setup_inputs(seed: int = 0) -> dict:
    seeds = jax.random.split(jax.random.key(seed), 8)
    rhs = bell_draw(seeds[0], (VARS, NODES), 1.0, 6.0, ((1, 32),), jnp.float32)
    precond = draw_precond(jax.random.fold_in(seeds[7], 71), 0)
    diag_blocks = draw_diag_blocks(jax.random.fold_in(seeds[7], 71), 0)
    off_blocks = bell_draw(seeds[3], (NBRS, VARS, VARS, NODES), 0.08, 0.5, ((3, 32),), jnp.float32)
    neighbours = touch_ends(jax.random.randint(seeds[4], (NBRS, NODES), 0, 2 * NODES_DEV), jax.random.fold_in(seeds[4], 1), 0, (2 * NODES_DEV) - 1).astype(jnp.int32)
    colours = draw_colours(jax.random.fold_in(seeds[7], 71), 0)
    send_lists = draw_send_lists(jax.random.fold_in(seeds[7], 71), 0)
    return dict(rhs=rhs, precond=precond, diag_blocks=diag_blocks, off_blocks=off_blocks, neighbours=neighbours, colours=colours, send_lists=send_lists)


def neighbour_sum(extended, neighbours, off_blocks):
    gathered = jnp.take(extended, neighbours, axis=1)
    return jnp.einsum("kabn,bkn->an", off_blocks, gathered, precision=lax.Precision.HIGHEST)


def apply_block(blocks, field):
    return jnp.einsum("abn,bn->an", blocks, field, precision=lax.Precision.HIGHEST)


def reference(rhs, precond, diag_blocks, off_blocks, neighbours, colours, send_lists):
    domains = N_DOM * N_SUB
    nodes_dev = rhs.shape[1] // domains
    slots = send_lists.shape[2] // domains
    rhs_dev = rhs.reshape(VARS, domains, nodes_dev).transpose(1, 0, 2)
    pre_dev = precond.reshape(VARS, VARS, domains, nodes_dev).transpose(2, 0, 1, 3)
    diag_dev = diag_blocks.reshape(VARS, VARS, domains, nodes_dev).transpose(2, 0, 1, 3)
    off_dev = off_blocks.reshape(NBRS, VARS, VARS, domains, nodes_dev).transpose(3, 0, 1, 2, 4)
    nbr_dev = neighbours.reshape(NBRS, domains, nodes_dev).transpose(1, 0, 2)
    col_dev = colours.reshape(domains, nodes_dev)
    send_dev = send_lists.reshape(4, 4, domains, slots).transpose(2, 0, 1, 3)

    def halo_of(field):
        outgoing = jax.vmap(lambda local, lists: local[:, lists])(field, send_dev)
        outgoing = outgoing.reshape(N_DOM, N_SUB, VARS, 4, 4, slots)
        arrived = jnp.stack([
            jnp.roll(outgoing[:, :, :, 0], 1, axis=0),
            jnp.roll(outgoing[:, :, :, 1], -1, axis=0),
            jnp.roll(outgoing[:, :, :, 2], 1, axis=1),
            jnp.roll(outgoing[:, :, :, 3], -1, axis=1)], axis=3)
        arrived = arrived.reshape(domains, VARS, 16 * slots)
        return jnp.concatenate([field, arrived], axis=2)

    def coupling(field):
        extended = halo_of(field)
        return jax.vmap(neighbour_sum)(extended, nbr_dev, off_dev)

    correction = jnp.zeros((domains, VARS, nodes_dev), jnp.float32)
    for colour in range(4):
        coupled = coupling(correction)
        candidate = jax.vmap(apply_block)(pre_dev, rhs_dev - coupled)
        correction = jnp.where((col_dev == colour)[:, None, :], candidate, correction)
    coupled = coupling(correction)
    residual_dev = rhs_dev - jax.vmap(apply_block)(diag_dev, correction) - coupled
    correction_out = correction.transpose(1, 0, 2).reshape(VARS, domains * nodes_dev)
    residual_out = residual_dev.transpose(1, 0, 2).reshape(VARS, domains * nodes_dev)
    return correction_out, residual_out
```

```python
import functools

import jax
import jax.numpy as jnp
from jax import lax
from jax.experimental import pallas as pl
from jax.experimental.pallas import tpu as pltpu
from jax.sharding import PartitionSpec as P

MESH = pl.DeviceIdType.MESH
COLOURS = 4
ROWS = 8
LANES = 128


def take(x, lane):
    return jnp.take_along_axis(x, lane, axis=1, mode="promise_in_bounds")


def spread(row):
    return jnp.broadcast_to(row, (ROWS, LANES))


def padded(x):
    return jnp.concatenate([x, jnp.zeros((ROWS - x.shape[0], LANES), x.dtype)], axis=0)


def row_sums(parts):
    row = lax.broadcasted_iota(jnp.int32, (ROWS, LANES), 0)
    first = []
    for j in range(2):
        x, y = parts[j], parts[j + 4]
        low = row < 4
        first.append(jnp.where(low, x, y) + pltpu.roll(jnp.where(low, y, x), 4, 0))
    for j in range(2, 4):
        x = parts[j]
        first.append(jnp.where(row < 4, x + pltpu.roll(x, 4, 0), 0.0))
    second = []
    for j in range(2):
        x, y = first[j], first[j + 2]
        second.append(jnp.where((row & 2) == 0, x + pltpu.roll(x, 6, 0), y + pltpu.roll(y, 2, 0)))
    x, y = second
    return jnp.where((row & 1) == 0, x + pltpu.roll(x, 7, 0), y + pltpu.roll(y, 1, 0))


def total(terms):
    while len(terms) > 1:
        terms = [sum(terms[i:i + 2][1:], terms[i]) for i in range(0, len(terms), 2)]
    return terms[0]


def kernel(
    n_dom, n_sub,
    rhs_hbm, pre_hbm, diag_hbm, off_hbm, nbr_hbm, send_hbm,
    corr_out, res_out,
    rhs, pre, diag, off, nbr, send_lists,
    off_p, pre_p, lane_of, code_of, outgoing, arrived,
    in_sem, send_sem, recv_sem,
):
    width = rhs.shape[0]
    nbrs = nbr.shape[0]
    blocks = rhs.shape[1] // LANES
    slots = send_lists.shape[2]

    loads = [
        pltpu.make_async_copy(src, dst, in_sem.at[i])
        for i, (src, dst) in enumerate([
            (send_hbm, send_lists), (rhs_hbm, rhs), (pre_hbm, pre),
            (nbr_hbm, nbr), (off_hbm, off), (diag_hbm, diag)])
    ]
    for load in loads:
        load.start()

    i, j = lax.axis_index("dom"), lax.axis_index("sub")
    targets = [
        (lax.rem(i + 1, n_dom), j), (lax.rem(i + n_dom - 1, n_dom), j),
        (i, lax.rem(j + 1, n_sub)), (i, lax.rem(j + n_sub - 1, n_sub)),
    ]
    barrier = pltpu.get_barrier_semaphore()
    for target in targets:
        pl.semaphore_signal(barrier, inc=1, device_id=target, device_id_type=MESH)

    lane = lax.broadcasted_iota(jnp.int32, (ROWS, LANES), 1)
    segment = lane // slots

    loads[0].wait()
    order = jnp.concatenate([send_lists[d] for d in range(4)], axis=1)
    order = padded(order)
    perm = [spread(order[c:c + 1]) for c in range(COLOURS)]

    def permuted(piece, c):
        got = take(padded(piece(0)), perm[c] & 127)
        for s in range(1, blocks):
            got = jnp.where((perm[c] >> 7) == s, take(padded(piece(s)), perm[c] & 127), got)
        return got

    def cut(s):
        return slice(s * LANES, (s + 1) * LANES)

    loads[1].wait()
    rhs_p = [permuted(lambda s: rhs[:, cut(s)], c) for c in range(COLOURS)]
    loads[2].wait()

    def permute_pre(c):
        for a in range(width):
            pre_p[c, a] = permuted(lambda s: pre[a, :, cut(s)], c)

    def apply_pre(c, field):
        return row_sums([pre_p[c, a] * field for a in range(width)])

    permute_pre(0)
    correction = [apply_pre(0, rhs_p[0])]
    outgoing[0] = correction[0]

    pl.semaphore_wait(barrier, 4)

    def copies(c):
        return [
            pltpu.make_async_remote_copy(
                src_ref=outgoing.at[c], dst_ref=arrived.at[c, d],
                send_sem=send_sem.at[c, d], recv_sem=recv_sem.at[c, d],
                device_id=targets[d], device_id_type=MESH)
            for d in range(4)
        ]

    flying = [copies(0)]
    for copy in flying[0]:
        copy.start()

    columns = order.T
    node = lax.broadcasted_iota(jnp.int32, (LANES, LANES), 1)
    lane_down = lax.broadcasted_iota(jnp.int32, (LANES, LANES), 0)
    place = []
    for s in range(blocks):
        hits = jnp.zeros((LANES, LANES), jnp.int32)
        for c in range(COLOURS):
            column = jnp.broadcast_to(columns[:, c:c + 1], (LANES, LANES))
            hits = jnp.where(column == node + s * LANES, lane_down + c * LANES, hits)
        place.append(spread(jnp.sum(hits, axis=0, keepdims=True)))

    loads[3].wait()
    for c in range(COLOURS):
        index = permuted(lambda s: nbr[:, cut(s)], c)
        local = take(place[0], index & 127)
        for s in range(1, blocks):
            local = jnp.where((index >> 7) == s, take(place[s], index & 127), local)
        outside = index >= LANES * blocks
        spot = index - LANES * blocks
        halo_lane = ((spot >> 7) & 3) * slots + (spot & (slots - 1))
        halo_code = 2 * ((spot >> 5) & 3) + 1
        lane_of[c] = jnp.where(outside, halo_lane, local & 127)
        code_of[c] = jnp.where(outside, halo_code, 2 * (local >> 7))

    loads[4].wait()
    live = lax.broadcasted_iota(jnp.int32, (ROWS, LANES), 0) < width

    def permute_off(c):
        def step(k, carry):
            for a in range(width):
                off_p[c, k, a] = permuted(lambda s: off[k, a, :, cut(s)], c)
            return carry
        lax.fori_loop(0, nbrs, step, 0)

    def contribution(c, sources):
        parts = [[] for _ in range(width)]
        for k in range(nbrs):
            where = spread(lane_of[c, k:k + 1])
            code = spread(code_of[c, k:k + 1])
            got = jnp.zeros((ROWS, LANES), jnp.float32)
            for number, block in sources:
                got = jnp.where(code == number, take(block, where), got)
            for a in range(width):
                parts[a].append(off_p[c, k, a] * got)
        return row_sums([total(part) for part in parts])

    halo = []

    def arrive(c):
        for copy in flying[c]:
            copy.wait_recv()
        got = arrived[c, 0]
        for d in range(1, 4):
            got = jnp.where(segment == d, arrived[c, d], got)
        halo.append(got)

    coupled = [jnp.zeros((ROWS, LANES), jnp.float32) for _ in range(COLOURS)]
    for c in range(1, COLOURS):
        permute_pre(c)
        permute_off(c)
        sources = [(2 * e, correction[e]) for e in range(c)]
        sources += [(2 * e + 1, halo[e]) for e in range(c - 1)]
        coupled[c] = contribution(c, sources)
        arrive(c - 1)
        coupled[c] += contribution(c, [(2 * c - 1, halo[c - 1])])
        correction.append(apply_pre(c, rhs_p[c] - coupled[c]))
        outgoing[c] = correction[c]
        flying.append(copies(c))
        for copy in flying[c]:
            copy.start()

    last = COLOURS - 1
    permute_off(0)
    for c in range(COLOURS):
        sources = [(2 * e, correction[e]) for e in range(c, COLOURS)]
        sources += [(2 * e + 1, halo[e]) for e in range(c, last)]
        coupled[c] += contribution(c, sources)

    def natural(fields, s):
        got = take(fields[0], place[s] & 127)
        for c in range(1, COLOURS):
            got = jnp.where((place[s] >> 7) == c, take(fields[c], place[s] & 127), got)
        return got

    loads[5].wait()
    base = []
    for s in range(blocks):
        field = natural(correction, s)
        corr_out[:, cut(s)] = field[:width]
        parts = [padded(diag[a, :, cut(s)]) * field for a in range(width)]
        base.append(padded(rhs[:, cut(s)]) - row_sums(parts))

    arrive(last)
    for c in range(COLOURS):
        coupled[c] += contribution(c, [(2 * last + 1, halo[last])])
    for s in range(blocks):
        res_out[:, cut(s)] = (base[s] - natural(coupled, s))[:width]

    for c in range(COLOURS):
        for copy in flying[c]:
            copy.wait_send()


def shards(n_dom, n_sub, rhs, precond, diag_blocks, off_blocks, neighbours, colours, send_lists):
    width, nodes = rhs.shape
    nbrs = neighbours.shape[0]
    blocks = nodes // LANES
    f32 = jnp.float32
    result = jax.ShapeDtypeStruct((width, nodes), f32)
    return pl.pallas_call(
        functools.partial(kernel, n_dom, n_sub),
        out_shape=(result, result),
        in_specs=[pl.BlockSpec(memory_space=pl.ANY)] * 6,
        out_specs=(pl.BlockSpec(memory_space=pltpu.VMEM),) * 2,
        scratch_shapes=[
            pltpu.VMEM(rhs.shape, f32),
            pltpu.VMEM(precond.shape, f32),
            pltpu.VMEM(diag_blocks.shape, f32),
            pltpu.VMEM(off_blocks.shape, f32),
            pltpu.VMEM(neighbours.shape, jnp.int32),
            pltpu.VMEM(send_lists.shape, jnp.int32),
            pltpu.VMEM((COLOURS, nbrs, width, ROWS, LANES), f32),
            pltpu.VMEM((COLOURS, width, ROWS, LANES), f32),
            pltpu.VMEM((COLOURS, ROWS, LANES), jnp.int32),
            pltpu.VMEM((COLOURS, ROWS, LANES), jnp.int32),
            pltpu.VMEM((COLOURS, ROWS, LANES), f32),
            pltpu.VMEM((COLOURS, 4, ROWS, LANES), f32),
            pltpu.SemaphoreType.DMA((6,)),
            pltpu.SemaphoreType.DMA((COLOURS, 4)),
            pltpu.SemaphoreType.DMA((COLOURS, 4)),
        ],
        compiler_params=pltpu.CompilerParams(
            collective_id=0, has_side_effects=True, vmem_limit_bytes=16 * 2**20),
    )(rhs, precond, diag_blocks, off_blocks, neighbours, send_lists)


def solution(mesh):
    both = ("dom", "sub")
    placed = (
        P(None, both),
        P(None, None, both),
        P(None, None, both),
        P(None, None, None, both),
        P(None, both),
        P(both),
        P(None, None, both),
    )
    return jax.shard_map(
        functools.partial(shards, mesh.shape["dom"], mesh.shape["sub"]),
        mesh=mesh,
        in_specs=placed,
        out_specs=(P(None, both), P(None, both)),
        check_vma=False,
    )
```

```python
import functools

import jax
import jax.numpy as jnp
from jax import lax
from jax.experimental import pallas as pl
from jax.experimental.pallas import tpu as pltpu
from jax.sharding import PartitionSpec as P

MESH = pl.DeviceIdType.MESH
COLOURS = 4
ROWS = 8
LANES = 128


def take(x, lane):
    return jnp.take_along_axis(x, lane, axis=1, mode="promise_in_bounds")


def spread(row):
    return jnp.broadcast_to(row, (ROWS, LANES))


def padded(x):
    return jnp.concatenate([x, jnp.zeros((ROWS - x.shape[0], LANES), x.dtype)], axis=0)


def row_sums(parts):
    row = lax.broadcasted_iota(jnp.int32, (ROWS, LANES), 0)
    first = []
    for j in range(2):
        x, y = parts[j], parts[j + 4]
        low = row < 4
        first.append(jnp.where(low, x, y) + pltpu.roll(jnp.where(low, y, x), 4, 0))
    for j in range(2, 4):
        x = parts[j]
        first.append(jnp.where(row < 4, x + pltpu.roll(x, 4, 0), 0.0))
    second = []
    for j in range(2):
        x, y = first[j], first[j + 2]
        second.append(jnp.where((row & 2) == 0, x + pltpu.roll(x, 6, 0), y + pltpu.roll(y, 2, 0)))
    x, y = second
    return jnp.where((row & 1) == 0, x + pltpu.roll(x, 7, 0), y + pltpu.roll(y, 1, 0))


def total(terms):
    while len(terms) > 1:
        terms = [sum(terms[i:i + 2][1:], terms[i]) for i in range(0, len(terms), 2)]
    return terms[0]


def kernel(
    n_dom, n_sub,
    rhs_hbm, pre_hbm, diag_hbm, off_hbm, nbr_hbm, send_hbm,
    both_out,
    rhs, pre, diag, off, nbr, send_lists,
    off_p, pre_p, lane_of, code_of, outgoing, arrived,
    in_sem, send_sem, recv_sem,
):
    corr_out, res_out = both_out.at[0], both_out.at[1]
    width = rhs.shape[0]
    nbrs = nbr.shape[0]
    blocks = rhs.shape[1] // LANES
    slots = send_lists.shape[2]

    loads = [
        pltpu.make_async_copy(src, dst, in_sem.at[i])
        for i, (src, dst) in enumerate([
            (send_hbm, send_lists), (rhs_hbm, rhs), (pre_hbm, pre),
            (nbr_hbm, nbr), (off_hbm, off), (diag_hbm, diag)])
    ]
    for load in loads:
        load.start()

    i, j = lax.axis_index("dom"), lax.axis_index("sub")
    targets = [
        (lax.rem(i + 1, n_dom), j), (lax.rem(i + n_dom - 1, n_dom), j),
        (i, lax.rem(j + 1, n_sub)), (i, lax.rem(j + n_sub - 1, n_sub)),
    ]
    barrier = pltpu.get_barrier_semaphore()
    for target in targets:
        pl.semaphore_signal(barrier, inc=1, device_id=target, device_id_type=MESH)

    lane = lax.broadcasted_iota(jnp.int32, (ROWS, LANES), 1)
    segment = lane // slots

    loads[0].wait()
    order = jnp.concatenate([send_lists[d] for d in range(4)], axis=1)
    order = padded(order)
    perm = [spread(order[c:c + 1]) for c in range(COLOURS)]

    def permuted(piece, c):
        got = take(padded(piece(0)), perm[c] & 127)
        for s in range(1, blocks):
            got = jnp.where((perm[c] >> 7) == s, take(padded(piece(s)), perm[c] & 127), got)
        return got

    def cut(s):
        return slice(s * LANES, (s + 1) * LANES)

    loads[1].wait()
    rhs_p = [permuted(lambda s: rhs[:, cut(s)], c) for c in range(COLOURS)]
    loads[2].wait()

    def permute_pre(c):
        for a in range(width):
            pre_p[c, a] = permuted(lambda s: pre[a, :, cut(s)], c)

    def apply_pre(c, field):
        return row_sums([pre_p[c, a] * field for a in range(width)])

    permute_pre(0)
    correction = [apply_pre(0, rhs_p[0])]
    outgoing[0] = correction[0]

    pl.semaphore_wait(barrier, 4)

    def copies(c):
        return [
            pltpu.make_async_remote_copy(
                src_ref=outgoing.at[c], dst_ref=arrived.at[c, d],
                send_sem=send_sem.at[c, d], recv_sem=recv_sem.at[c, d],
                device_id=targets[d], device_id_type=MESH)
            for d in range(4)
        ]

    flying = [copies(0)]
    for copy in flying[0]:
        copy.start()

    columns = order.T
    node = lax.broadcasted_iota(jnp.int32, (LANES, LANES), 1)
    lane_down = lax.broadcasted_iota(jnp.int32, (LANES, LANES), 0)
    place = []
    for s in range(blocks):
        hits = jnp.zeros((LANES, LANES), jnp.int32)
        for c in range(COLOURS):
            column = jnp.broadcast_to(columns[:, c:c + 1], (LANES, LANES))
            hits = jnp.where(column == node + s * LANES, lane_down + c * LANES, hits)
        place.append(spread(jnp.sum(hits, axis=0, keepdims=True)))

    loads[3].wait()
    for c in range(COLOURS):
        index = permuted(lambda s: nbr[:, cut(s)], c)
        local = take(place[0], index & 127)
        for s in range(1, blocks):
            local = jnp.where((index >> 7) == s, take(place[s], index & 127), local)
        outside = index >= LANES * blocks
        spot = index - LANES * blocks
        halo_lane = ((spot >> 7) & 3) * slots + (spot & (slots - 1))
        halo_code = 2 * ((spot >> 5) & 3) + 1
        lane_of[c] = jnp.where(outside, halo_lane, local & 127)
        code_of[c] = jnp.where(outside, halo_code, 2 * (local >> 7))

    loads[4].wait()
    live = lax.broadcasted_iota(jnp.int32, (ROWS, LANES), 0) < width

    def permute_off(c):
        def step(k, carry):
            for a in range(width):
                off_p[c, k, a] = permuted(lambda s: off[k, a, :, cut(s)], c)
            return carry
        lax.fori_loop(0, nbrs, step, 0)

    def contribution(c, sources):
        parts = [[] for _ in range(width)]
        for k in range(nbrs):
            where = spread(lane_of[c, k:k + 1])
            code = spread(code_of[c, k:k + 1])
            got = jnp.zeros((ROWS, LANES), jnp.float32)
            for number, block in sources:
                got = jnp.where(code == number, take(block, where), got)
            for a in range(width):
                parts[a].append(off_p[c, k, a] * got)
        return row_sums([total(part) for part in parts])

    halo = []

    def arrive(c):
        for copy in flying[c]:
            copy.wait_recv()
        got = arrived[c, 0]
        for d in range(1, 4):
            got = jnp.where(segment == d, arrived[c, d], got)
        halo.append(got)

    coupled = [jnp.zeros((ROWS, LANES), jnp.float32) for _ in range(COLOURS)]
    for c in range(1, COLOURS):
        permute_pre(c)
        permute_off(c)
        sources = [(2 * e, correction[e]) for e in range(c)]
        sources += [(2 * e + 1, halo[e]) for e in range(c - 1)]
        coupled[c] = contribution(c, sources)
        arrive(c - 1)
        coupled[c] += contribution(c, [(2 * c - 1, halo[c - 1])])
        correction.append(apply_pre(c, rhs_p[c] - coupled[c]))
        outgoing[c] = correction[c]
        flying.append(copies(c))
        for copy in flying[c]:
            copy.start()

    last = COLOURS - 1
    permute_off(0)
    for c in range(COLOURS):
        sources = [(2 * e, correction[e]) for e in range(c, COLOURS)]
        sources += [(2 * e + 1, halo[e]) for e in range(c, last)]
        coupled[c] += contribution(c, sources)

    def natural(fields, s):
        got = take(fields[0], place[s] & 127)
        for c in range(1, COLOURS):
            got = jnp.where((place[s] >> 7) == c, take(fields[c], place[s] & 127), got)
        return got

    loads[5].wait()
    base = []
    for s in range(blocks):
        field = natural(correction, s)
        corr_out[:, cut(s)] = field[:width]
        parts = [padded(diag[a, :, cut(s)]) * field for a in range(width)]
        base.append(padded(rhs[:, cut(s)]) - row_sums(parts))

    arrive(last)
    for c in range(COLOURS):
        coupled[c] += contribution(c, [(2 * last + 1, halo[last])])
    for s in range(blocks):
        res_out[:, cut(s)] = (base[s] - natural(coupled, s))[:width]

    for c in range(COLOURS):
        for copy in flying[c]:
            copy.wait_send()


def shards(n_dom, n_sub, rhs, precond, diag_blocks, off_blocks, neighbours, colours, send_lists):
    width, nodes = rhs.shape
    nbrs = neighbours.shape[0]
    f32 = jnp.float32
    arrays = (rhs, precond, diag_blocks, off_blocks, neighbours, send_lists)
    both = pl.pallas_call(
        functools.partial(kernel, n_dom, n_sub),
        out_shape=jax.ShapeDtypeStruct((2, width, nodes), f32),
        in_specs=[pl.BlockSpec(memory_space=pltpu.HBM)] * 6,
        out_specs=pl.BlockSpec(memory_space=pltpu.VMEM),
        scratch_shapes=[
            pltpu.VMEM(rhs.shape, f32),
            pltpu.VMEM(precond.shape, f32),
            pltpu.VMEM(diag_blocks.shape, f32),
            pltpu.VMEM(off_blocks.shape, f32),
            pltpu.VMEM(neighbours.shape, jnp.int32),
            pltpu.VMEM(send_lists.shape, jnp.int32),
            pltpu.VMEM((COLOURS, nbrs, width, ROWS, LANES), f32),
            pltpu.VMEM((COLOURS, width, ROWS, LANES), f32),
            pltpu.VMEM((COLOURS, ROWS, LANES), jnp.int32),
            pltpu.VMEM((COLOURS, ROWS, LANES), jnp.int32),
            pltpu.VMEM((COLOURS, ROWS, LANES), f32),
            pltpu.VMEM((COLOURS, 4, ROWS, LANES), f32),
            pltpu.SemaphoreType.DMA((6,)),
            pltpu.SemaphoreType.DMA((COLOURS, 4)),
            pltpu.SemaphoreType.DMA((COLOURS, 4)),
        ],
        compiler_params=pltpu.CompilerParams(
            collective_id=0, has_side_effects=True, vmem_limit_bytes=16 * 2**20),
    )(*[pltpu.with_memory_space_constraint(x, pltpu.HBM) for x in arrays])
    return both[0], both[1]


def solution(mesh):
    both = ("dom", "sub")
    placed = (
        P(None, both),
        P(None, None, both),
        P(None, None, both),
        P(None, None, None, both),
        P(None, both),
        P(both),
        P(None, None, both),
    )
    return jax.shard_map(
        functools.partial(shards, mesh.shape["dom"], mesh.shape["sub"]),
        mesh=mesh,
        in_specs=placed,
        out_specs=(P(None, both), P(None, both)),
        check_vma=False,
    )
```

```python
import functools

import jax
import jax.numpy as jnp
from jax import lax
from jax.experimental import pallas as pl
from jax.experimental.pallas import tpu as pltpu
from jax.sharding import PartitionSpec as P

MESH = pl.DeviceIdType.MESH
COLOURS = 4
ROWS = 8
LANES = 128


def take(x, lane):
    return jnp.take_along_axis(x, lane, axis=1, mode="promise_in_bounds")


def spread(row):
    return jnp.broadcast_to(row, (ROWS, LANES))


def padded(x):
    return jnp.concatenate([x, jnp.zeros((ROWS - x.shape[0], LANES), x.dtype)], axis=0)


def row_sums(parts):
    row = lax.broadcasted_iota(jnp.int32, (ROWS, LANES), 0)
    first = []
    for j in range(2):
        x, y = parts[j], parts[j + 4]
        low = row < 4
        first.append(jnp.where(low, x, y) + pltpu.roll(jnp.where(low, y, x), 4, 0))
    for j in range(2, 4):
        x = parts[j]
        first.append(jnp.where(row < 4, x + pltpu.roll(x, 4, 0), 0.0))
    second = []
    for j in range(2):
        x, y = first[j], first[j + 2]
        second.append(jnp.where((row & 2) == 0, x + pltpu.roll(x, 6, 0), y + pltpu.roll(y, 2, 0)))
    x, y = second
    return jnp.where((row & 1) == 0, x + pltpu.roll(x, 7, 0), y + pltpu.roll(y, 1, 0))


def total(terms):
    while len(terms) > 1:
        terms = [sum(terms[i:i + 2][1:], terms[i]) for i in range(0, len(terms), 2)]
    return terms[0]


def kernel(
    n_dom, n_sub,
    rhs_hbm, pre_hbm, diag_hbm, off_hbm, nbr_hbm, send_hbm,
    both_out,
    rhs, pre, diag, off, nbr, send_lists,
    off_p, pre_p, lane_of, code_of, outgoing, arrived,
    kit, kit_in, spots, spots_in, rest, rest_in,
    in_sem, send_sem, recv_sem, kit_send_sem, kit_recv_sem,
):
    corr_out, res_out = both_out.at[0], both_out.at[1]
    width = rhs.shape[0]
    nbrs = nbr.shape[0]
    blocks = rhs.shape[1] // LANES
    slots = send_lists.shape[2]
    groups = pl.cdiv(nbrs, 4)

    loads = [
        pltpu.make_async_copy(src, dst, in_sem.at[i])
        for i, (src, dst) in enumerate([
            (send_hbm, send_lists), (rhs_hbm, rhs), (pre_hbm, pre),
            (nbr_hbm, nbr), (off_hbm, off), (diag_hbm, diag)])
    ]
    for load in loads:
        load.start()

    i, j = lax.axis_index("dom"), lax.axis_index("sub")
    targets = [
        (lax.rem(i + 1, n_dom), j), (lax.rem(i + n_dom - 1, n_dom), j),
        (i, lax.rem(j + 1, n_sub)), (i, lax.rem(j + n_sub - 1, n_sub)),
    ]
    barrier = pltpu.get_barrier_semaphore()
    for target in targets:
        pl.semaphore_signal(barrier, inc=1, device_id=target, device_id_type=MESH)

    lane = lax.broadcasted_iota(jnp.int32, (ROWS, LANES), 1)
    segment = lane // slots

    loads[0].wait()
    order = jnp.concatenate([send_lists[d] for d in range(4)], axis=1)
    order = padded(order)
    perm = [spread(order[c:c + 1]) for c in range(COLOURS)]

    def permuted(piece, c):
        got = take(padded(piece(0)), perm[c] & 127)
        for s in range(1, blocks):
            got = jnp.where((perm[c] >> 7) == s, take(padded(piece(s)), perm[c] & 127), got)
        return got

    def cut(s):
        return slice(s * LANES, (s + 1) * LANES)

    loads[1].wait()
    rhs_p = [permuted(lambda s: rhs[:, cut(s)], c) for c in range(COLOURS)]
    loads[2].wait()

    def permute_pre(c):
        for a in range(width):
            pre_p[c, a] = permuted(lambda s: pre[a, :, cut(s)], c)

    def apply_pre(c, field):
        return row_sums([pre_p[c, a] * field for a in range(width)])

    permute_pre(0)
    correction = [apply_pre(0, rhs_p[0])]
    outgoing[0] = correction[0]

    pl.semaphore_wait(barrier, 4)

    def send(c, directions):
        started = {
            d: pltpu.make_async_remote_copy(
                src_ref=outgoing.at[c], dst_ref=arrived.at[c, d],
                send_sem=send_sem.at[c, d], recv_sem=recv_sem.at[c, d],
                device_id=targets[d], device_id_type=MESH)
            for d in directions
        }
        for copy in started.values():
            copy.start()
        return started

    flying = [send(0, range(4))]
    kit_copies = [
        pltpu.make_async_remote_copy(
            src_ref=src, dst_ref=dst, send_sem=kit_send_sem.at[n], recv_sem=kit_recv_sem.at[n],
            device_id=targets[0], device_id_type=MESH)
        for n, (src, dst) in enumerate([(kit, kit_in), (spots, spots_in), (rest, rest_in)])
    ]

    columns = order.T
    node = lax.broadcasted_iota(jnp.int32, (LANES, LANES), 1)
    lane_down = lax.broadcasted_iota(jnp.int32, (LANES, LANES), 0)
    place = []
    for s in range(blocks):
        hits = jnp.zeros((LANES, LANES), jnp.int32)
        for c in range(COLOURS):
            column = jnp.broadcast_to(columns[:, c:c + 1], (LANES, LANES))
            hits = jnp.where(column == node + s * LANES, lane_down + c * LANES, hits)
        place.append(spread(jnp.sum(hits, axis=0, keepdims=True)))

    loads[3].wait()
    for c in range(COLOURS):
        index = permuted(lambda s: nbr[:, cut(s)], c)
        local = take(place[0], index & 127)
        for s in range(1, blocks):
            local = jnp.where((index >> 7) == s, take(place[s], index & 127), local)
        outside = index >= LANES * blocks
        spot = index - LANES * blocks
        halo_lane = ((spot >> 7) & 3) * slots + (spot & (slots - 1))
        halo_code = 2 * ((spot >> 5) & 3) + 1
        lane_of[c] = jnp.where(outside, halo_lane, local & 127)
        code_of[c] = jnp.where(outside, halo_code, 2 * (local >> 7))

    loads[4].wait()
    live = lax.broadcasted_iota(jnp.int32, (ROWS, LANES), 0) < width

    def permute_off(c):
        def step(k, carry):
            for a in range(width):
                off_p[c, k, a] = permuted(lambda s: off[k, a, :, cut(s)], c)
            return carry
        lax.fori_loop(0, nbrs, step, 0)

    def contribution(c, sources):
        parts = [[] for _ in range(width)]
        for k in range(nbrs):
            where = spread(lane_of[c, k:k + 1])
            code = spread(code_of[c, k:k + 1])
            got = jnp.zeros((ROWS, LANES), jnp.float32)
            for number, block in sources:
                got = jnp.where(code == number, take(block, where), got)
            for a in range(width):
                parts[a].append(off_p[c, k, a] * got)
        return row_sums([total(part) for part in parts])

    halo = []

    def arrive(c, got=None):
        for copy in flying[c].values():
            copy.wait_recv()
        for d in flying[c]:
            got = arrived[c, d] if got is None else jnp.where(segment == d, arrived[c, d], got)
        halo.append(got)

    def send_kit():
        mine = (code_of[1] == 1) & (lane_of[1] // slots == 1)
        reads = jnp.where(mine, lane_of[1], -1)
        for g in range(groups):
            spot = jnp.full((ROWS, LANES), -1, jnp.int32)
            for q in range(min(4, nbrs - 4 * g)):
                k = 4 * g + q
                moved = pltpu.roll(spread(reads[k:k + 1]), q * slots, 1)
                spot = jnp.where(segment == q, moved, spot)
            spots[g] = spot
        for a in range(width):
            for g in range(groups):
                tile = jnp.zeros((ROWS, LANES), jnp.float32)
                for q in range(min(4, nbrs - 4 * g)):
                    moved = pltpu.roll(off_p[1, 4 * g + q, a], q * slots, 1)
                    tile = jnp.where(segment == q, moved, tile)
                kit[a * groups + g] = tile
            kit[width * groups + a] = pre_p[1, a]
        kit_copies[0].start()
        kit_copies[1].start()

    def from_kit():
        kit_copies[0].wait_recv()
        kit_copies[1].wait_recv()
        reads = []
        for g in range(groups):
            spot = spots_in[g]
            reads.append(jnp.where(spot >= 0, take(correction[0], spot & 127), 0.0))
        parts = [
            total([kit_in[a * groups + g] * reads[g] for g in range(groups)]) for a in range(width)
        ]
        coupling = row_sums(parts)
        coupling += pltpu.roll(coupling, 2 * slots, 1)
        coupling += pltpu.roll(coupling, slots, 1)
        kit_copies[2].wait_recv()
        field = rest_in[...] - coupling
        return row_sums([kit_in[width * groups + a] * field for a in range(width)])

    coupled = [jnp.zeros((ROWS, LANES), jnp.float32) for _ in range(COLOURS)]
    for c in range(1, COLOURS):
        permute_pre(c)
        permute_off(c)
        sources = [(2 * e, correction[e]) for e in range(c)]
        sources += [(2 * e + 1, halo[e]) for e in range(c - 1)]
        coupled[c] = contribution(c, sources)
        if c == 1:
            send_kit()
            others = jnp.zeros((ROWS, LANES), jnp.float32)
            for d in (2, 3, 0):
                flying[0][d].wait_recv()
                others = jnp.where(segment == d, arrived[0, d], others)
            coupled[1] += contribution(1, [(1, others)])
            rest[...] = rhs_p[1] - coupled[1]
            kit_copies[2].start()
            flying[0][1].wait_recv()
            upper = jnp.where(segment == 1, arrived[0, 1], 0.0)
            halo.append(others + upper)
            coupled[1] += contribution(1, [(1, upper)])
        else:
            arrive(c - 1, from_kit() if c == 2 else None)
            coupled[c] += contribution(c, [(2 * c - 1, halo[c - 1])])
        correction.append(apply_pre(c, rhs_p[c] - coupled[c]))
        outgoing[c] = correction[c]
        flying.append(send(c, range(1, 4) if c == 1 else range(4)))

    last = COLOURS - 1
    permute_off(0)
    for c in range(COLOURS):
        sources = [(2 * e, correction[e]) for e in range(c, COLOURS)]
        sources += [(2 * e + 1, halo[e]) for e in range(c, last)]
        coupled[c] += contribution(c, sources)

    def natural(fields, s):
        got = take(fields[0], place[s] & 127)
        for c in range(1, COLOURS):
            got = jnp.where((place[s] >> 7) == c, take(fields[c], place[s] & 127), got)
        return got

    loads[5].wait()
    base = []
    for s in range(blocks):
        field = natural(correction, s)
        corr_out[:, cut(s)] = field[:width]
        parts = [padded(diag[a, :, cut(s)]) * field for a in range(width)]
        base.append(padded(rhs[:, cut(s)]) - row_sums(parts))

    arrive(last)
    for c in range(COLOURS):
        coupled[c] += contribution(c, [(2 * last + 1, halo[last])])
    for s in range(blocks):
        res_out[:, cut(s)] = (base[s] - natural(coupled, s))[:width]

    for c in range(COLOURS):
        for copy in flying[c].values():
            copy.wait_send()
    for copy in kit_copies:
        copy.wait_send()


def shards(n_dom, n_sub, rhs, precond, diag_blocks, off_blocks, neighbours, colours, send_lists):
    width, nodes = rhs.shape
    nbrs = neighbours.shape[0]
    f32 = jnp.float32
    groups = pl.cdiv(nbrs, 4)
    tiles = width * groups + width
    arrays = (rhs, precond, diag_blocks, off_blocks, neighbours, send_lists)
    both = pl.pallas_call(
        functools.partial(kernel, n_dom, n_sub),
        out_shape=jax.ShapeDtypeStruct((2, width, nodes), f32),
        in_specs=[pl.BlockSpec(memory_space=pltpu.HBM)] * 6,
        out_specs=pl.BlockSpec(memory_space=pltpu.VMEM),
        scratch_shapes=[
            pltpu.VMEM(rhs.shape, f32),
            pltpu.VMEM(precond.shape, f32),
            pltpu.VMEM(diag_blocks.shape, f32),
            pltpu.VMEM(off_blocks.shape, f32),
            pltpu.VMEM(neighbours.shape, jnp.int32),
            pltpu.VMEM(send_lists.shape, jnp.int32),
            pltpu.VMEM((COLOURS, nbrs, width, ROWS, LANES), f32),
            pltpu.VMEM((COLOURS, width, ROWS, LANES), f32),
            pltpu.VMEM((COLOURS, ROWS, LANES), jnp.int32),
            pltpu.VMEM((COLOURS, ROWS, LANES), jnp.int32),
            pltpu.VMEM((COLOURS, ROWS, LANES), f32),
            pltpu.VMEM((COLOURS, 4, ROWS, LANES), f32),
            *[pltpu.VMEM((tiles, ROWS, LANES), f32)] * 2,
            *[pltpu.VMEM((groups, ROWS, LANES), jnp.int32)] * 2,
            *[pltpu.VMEM((ROWS, LANES), f32)] * 2,
            pltpu.SemaphoreType.DMA((6,)),
            pltpu.SemaphoreType.DMA((COLOURS, 4)),
            pltpu.SemaphoreType.DMA((COLOURS, 4)),
            pltpu.SemaphoreType.DMA((3,)),
            pltpu.SemaphoreType.DMA((3,)),
        ],
        compiler_params=pltpu.CompilerParams(
            collective_id=0, has_side_effects=True, vmem_limit_bytes=16 * 2**20),
    )(*[pltpu.with_memory_space_constraint(x, pltpu.HBM) for x in arrays])
    return both[0], both[1]


def solution(mesh):
    both = ("dom", "sub")
    placed = (
        P(None, both),
        P(None, None, both),
        P(None, None, both),
        P(None, None, None, both),
        P(None, both),
        P(both),
        P(None, None, both),
    )
    return jax.shard_map(
        functools.partial(shards, mesh.shape["dom"], mesh.shape["sub"]),
        mesh=mesh,
        in_specs=placed,
        out_specs=(P(None, both), P(None, both)),
        check_vma=False,
    )
```

```python
import functools

import jax
import jax.numpy as jnp
from jax import lax
from jax.experimental import pallas as pl
from jax.experimental.pallas import tpu as pltpu
from jax.sharding import PartitionSpec as P

MESH = pl.DeviceIdType.MESH
COLOURS = 4
ROWS = 8
LANES = 128
KITS = {1: 0, 3: 1}


def take(x, lane):
    return jnp.take_along_axis(x, lane, axis=1, mode="promise_in_bounds")


def spread(row):
    return jnp.broadcast_to(row, (ROWS, LANES))


def padded(x):
    return jnp.concatenate([x, jnp.zeros((ROWS - x.shape[0], LANES), x.dtype)], axis=0)


def row_sums(parts):
    row = lax.broadcasted_iota(jnp.int32, (ROWS, LANES), 0)
    first = []
    for j in range(2):
        x, y = parts[j], parts[j + 4]
        low = row < 4
        first.append(jnp.where(low, x, y) + pltpu.roll(jnp.where(low, y, x), 4, 0))
    for j in range(2, 4):
        x = parts[j]
        first.append(jnp.where(row < 4, x + pltpu.roll(x, 4, 0), 0.0))
    second = []
    for j in range(2):
        x, y = first[j], first[j + 2]
        second.append(jnp.where((row & 2) == 0, x + pltpu.roll(x, 6, 0), y + pltpu.roll(y, 2, 0)))
    x, y = second
    return jnp.where((row & 1) == 0, x + pltpu.roll(x, 7, 0), y + pltpu.roll(y, 1, 0))


def total(terms):
    while len(terms) > 1:
        terms = [sum(terms[i:i + 2][1:], terms[i]) for i in range(0, len(terms), 2)]
    return terms[0]


def kernel(
    n_dom, n_sub,
    rhs_hbm, pre_hbm, diag_hbm, off_hbm, nbr_hbm, send_hbm,
    both_out,
    rhs, pre, diag, off, nbr, send_lists,
    off_p, pre_p, lane_of, code_of, outgoing, arrived,
    kit, kit_in, spots, spots_in, rest, rest_in,
    in_sem, send_sem, recv_sem, kit_send_sem, kit_recv_sem,
):
    corr_out, res_out = both_out.at[0], both_out.at[1]
    width = rhs.shape[0]
    nbrs = nbr.shape[0]
    blocks = rhs.shape[1] // LANES
    slots = send_lists.shape[2]
    groups = pl.cdiv(nbrs, 4)

    loads = [
        pltpu.make_async_copy(src, dst, in_sem.at[i])
        for i, (src, dst) in enumerate([
            (send_hbm, send_lists), (rhs_hbm, rhs), (pre_hbm, pre),
            (nbr_hbm, nbr), (off_hbm, off), (diag_hbm, diag)])
    ]
    for load in loads:
        load.start()

    i, j = lax.axis_index("dom"), lax.axis_index("sub")
    targets = [
        (lax.rem(i + 1, n_dom), j), (lax.rem(i + n_dom - 1, n_dom), j),
        (i, lax.rem(j + 1, n_sub)), (i, lax.rem(j + n_sub - 1, n_sub)),
    ]
    barrier = pltpu.get_barrier_semaphore()
    for target in targets:
        pl.semaphore_signal(barrier, inc=1, device_id=target, device_id_type=MESH)

    lane = lax.broadcasted_iota(jnp.int32, (ROWS, LANES), 1)
    segment = lane // slots

    loads[0].wait()
    order = jnp.concatenate([send_lists[d] for d in range(4)], axis=1)
    order = padded(order)
    perm = [spread(order[c:c + 1]) for c in range(COLOURS)]

    def permuted(piece, c):
        got = take(padded(piece(0)), perm[c] & 127)
        for s in range(1, blocks):
            got = jnp.where((perm[c] >> 7) == s, take(padded(piece(s)), perm[c] & 127), got)
        return got

    def cut(s):
        return slice(s * LANES, (s + 1) * LANES)

    loads[1].wait()
    rhs_p = [permuted(lambda s: rhs[:, cut(s)], 0)]
    loads[2].wait()

    def permute_pre(c):
        for a in range(width):
            pre_p[c, a] = permuted(lambda s: pre[a, :, cut(s)], c)

    def apply_pre(c, field):
        return row_sums([pre_p[c, a] * field for a in range(width)])

    permute_pre(0)
    correction = [apply_pre(0, rhs_p[0])]
    outgoing[0] = correction[0]

    pl.semaphore_wait(barrier, 4)

    def send(c, directions):
        started = {
            d: pltpu.make_async_remote_copy(
                src_ref=outgoing.at[c], dst_ref=arrived.at[c, d],
                send_sem=send_sem.at[c, d], recv_sem=recv_sem.at[c, d],
                device_id=targets[d], device_id_type=MESH)
            for d in directions
        }
        for copy in started.values():
            copy.start()
        return started

    flying = [send(0, range(4))]
    kit_copies = {
        c: [
            pltpu.make_async_remote_copy(
                src_ref=src.at[d], dst_ref=dst.at[d],
                send_sem=kit_send_sem.at[d, n], recv_sem=kit_recv_sem.at[d, n],
                device_id=targets[d], device_id_type=MESH)
            for n, (src, dst) in enumerate([(kit, kit_in), (spots, spots_in), (rest, rest_in)])
        ]
        for c, d in KITS.items()
    }

    rhs_p += [permuted(lambda s: rhs[:, cut(s)], c) for c in range(1, COLOURS)]

    columns = order.T
    node = lax.broadcasted_iota(jnp.int32, (LANES, LANES), 1)
    lane_down = lax.broadcasted_iota(jnp.int32, (LANES, LANES), 0)
    place = []
    for s in range(blocks):
        hits = jnp.zeros((LANES, LANES), jnp.int32)
        for c in range(COLOURS):
            column = jnp.broadcast_to(columns[:, c:c + 1], (LANES, LANES))
            hits = jnp.where(column == node + s * LANES, lane_down + c * LANES, hits)
        place.append(spread(jnp.sum(hits, axis=0, keepdims=True)))

    loads[3].wait()
    for c in range(COLOURS):
        index = permuted(lambda s: nbr[:, cut(s)], c)
        local = take(place[0], index & 127)
        for s in range(1, blocks):
            local = jnp.where((index >> 7) == s, take(place[s], index & 127), local)
        outside = index >= LANES * blocks
        spot = index - LANES * blocks
        halo_lane = ((spot >> 7) & 3) * slots + (spot & (slots - 1))
        halo_code = 2 * ((spot >> 5) & 3) + 1
        lane_of[c] = jnp.where(outside, halo_lane, local & 127)
        code_of[c] = jnp.where(outside, halo_code, 2 * (local >> 7))

    loads[4].wait()
    live = lax.broadcasted_iota(jnp.int32, (ROWS, LANES), 0) < width

    def permute_off(c):
        def step(k, carry):
            for a in range(width):
                off_p[c, k, a] = permuted(lambda s: off[k, a, :, cut(s)], c)
            return carry
        lax.fori_loop(0, nbrs, step, 0)

    def contribution(c, sources):
        parts = [[] for _ in range(width)]
        for k in range(nbrs):
            where = spread(lane_of[c, k:k + 1])
            code = spread(code_of[c, k:k + 1])
            got = jnp.zeros((ROWS, LANES), jnp.float32)
            for number, block in sources:
                got = jnp.where(code == number, take(block, where), got)
            for a in range(width):
                parts[a].append(off_p[c, k, a] * got)
        return row_sums([total(part) for part in parts])

    halo = []

    def arrive(c, got=None):
        for copy in flying[c].values():
            copy.wait_recv()
        for d in flying[c]:
            got = arrived[c, d] if got is None else jnp.where(segment == d, arrived[c, d], got)
        halo.append(got)

    def send_kit(c):
        d = KITS[c]
        mine = (code_of[c] == 2 * c - 1) & (lane_of[c] // slots == 1 - d)
        reads = jnp.where(mine, lane_of[c], -1)

        def moved(x, q):
            shift = (q - d) % 4 * slots
            return pltpu.roll(x, shift, 1) if shift else x

        for g in range(groups):
            spot = jnp.full((ROWS, LANES), -1, jnp.int32)
            for q in range(min(4, nbrs - 4 * g)):
                k = 4 * g + q
                spot = jnp.where(segment == q, moved(spread(reads[k:k + 1]), q), spot)
            spots[d, g] = spot
        for a in range(width):
            for g in range(groups):
                tile = jnp.zeros((ROWS, LANES), jnp.float32)
                for q in range(min(4, nbrs - 4 * g)):
                    tile = jnp.where(segment == q, moved(off_p[c, 4 * g + q, a], q), tile)
                kit[d, a * groups + g] = tile
            kit[d, width * groups + a] = pre_p[c, a]
        kit_copies[c][0].start()
        kit_copies[c][1].start()

    def from_kit(c):
        d = KITS[c]
        kit_copies[c][0].wait_recv()
        kit_copies[c][1].wait_recv()
        reads = []
        for g in range(groups):
            spot = spots_in[d, g]
            reads.append(jnp.where(spot >= 0, take(correction[c - 1], spot & 127), 0.0))
        parts = [
            total([kit_in[d, a * groups + g] * reads[g] for g in range(groups)]) for a in range(width)
        ]
        coupling = row_sums(parts)
        coupling += pltpu.roll(coupling, 2 * slots, 1)
        coupling += pltpu.roll(coupling, slots, 1)
        kit_copies[c][2].wait_recv()
        field = rest_in[d] - coupling
        return row_sums([kit_in[d, width * groups + a] * field for a in range(width)])

    coupled = [jnp.zeros((ROWS, LANES), jnp.float32) for _ in range(COLOURS)]
    for c in range(1, COLOURS):
        permute_pre(c)
        permute_off(c)
        sources = [(2 * e, correction[e]) for e in range(c)]
        sources += [(2 * e + 1, halo[e]) for e in range(c - 1)]
        coupled[c] = contribution(c, sources)
        known = from_kit(c - 1) if c - 1 in KITS else None
        if c in KITS:
            send_kit(c)
            d = KITS[c]
            others = jnp.zeros((ROWS, LANES), jnp.float32) if known is None else known
            for e in flying[c - 1]:
                if e != 1 - d:
                    flying[c - 1][e].wait_recv()
                    others = jnp.where(segment == e, arrived[c - 1, e], others)
            others = jnp.where(segment == 1 - d, 0.0, others)
            coupled[c] += contribution(c, [(2 * c - 1, others)])
            rest[d] = rhs_p[c] - coupled[c]
            kit_copies[c][2].start()
            flying[c - 1][1 - d].wait_recv()
            back = jnp.where(segment == 1 - d, arrived[c - 1, 1 - d], 0.0)
            halo.append(others + back)
            coupled[c] += contribution(c, [(2 * c - 1, back)])
        else:
            arrive(c - 1, known)
            coupled[c] += contribution(c, [(2 * c - 1, halo[c - 1])])
        correction.append(apply_pre(c, rhs_p[c] - coupled[c]))
        outgoing[c] = correction[c]
        flying.append(send(c, [d for d in range(4) if d != KITS.get(c)]))

    last = COLOURS - 1
    permute_off(0)
    for c in range(COLOURS):
        sources = [(2 * e, correction[e]) for e in range(c, COLOURS)]
        sources += [(2 * e + 1, halo[e]) for e in range(c, last)]
        coupled[c] += contribution(c, sources)

    def natural(fields, s):
        got = take(fields[0], place[s] & 127)
        for c in range(1, COLOURS):
            got = jnp.where((place[s] >> 7) == c, take(fields[c], place[s] & 127), got)
        return got

    loads[5].wait()
    base = []
    for s in range(blocks):
        field = natural(correction, s)
        corr_out[:, cut(s)] = field[:width]
        parts = [padded(diag[a, :, cut(s)]) * field for a in range(width)]
        base.append(padded(rhs[:, cut(s)]) - row_sums(parts))

    arrive(last, from_kit(last) if last in KITS else None)
    for c in range(COLOURS):
        coupled[c] += contribution(c, [(2 * last + 1, halo[last])])
    for s in range(blocks):
        res_out[:, cut(s)] = (base[s] - natural(coupled, s))[:width]

    for c in range(COLOURS):
        for copy in flying[c].values():
            copy.wait_send()
    for started in kit_copies.values():
        for copy in started:
            copy.wait_send()


def shards(n_dom, n_sub, rhs, precond, diag_blocks, off_blocks, neighbours, colours, send_lists):
    width, nodes = rhs.shape
    nbrs = neighbours.shape[0]
    f32 = jnp.float32
    groups = pl.cdiv(nbrs, 4)
    tiles = width * groups + width
    arrays = (rhs, precond, diag_blocks, off_blocks, neighbours, send_lists)
    both = pl.pallas_call(
        functools.partial(kernel, n_dom, n_sub),
        out_shape=jax.ShapeDtypeStruct((2, width, nodes), f32),
        in_specs=[pl.BlockSpec(memory_space=pltpu.HBM)] * 6,
        out_specs=pl.BlockSpec(memory_space=pltpu.VMEM),
        scratch_shapes=[
            pltpu.VMEM(rhs.shape, f32),
            pltpu.VMEM(precond.shape, f32),
            pltpu.VMEM(diag_blocks.shape, f32),
            pltpu.VMEM(off_blocks.shape, f32),
            pltpu.VMEM(neighbours.shape, jnp.int32),
            pltpu.VMEM(send_lists.shape, jnp.int32),
            pltpu.VMEM((COLOURS, nbrs, width, ROWS, LANES), f32),
            pltpu.VMEM((COLOURS, width, ROWS, LANES), f32),
            pltpu.VMEM((COLOURS, ROWS, LANES), jnp.int32),
            pltpu.VMEM((COLOURS, ROWS, LANES), jnp.int32),
            pltpu.VMEM((COLOURS, ROWS, LANES), f32),
            pltpu.VMEM((COLOURS, 4, ROWS, LANES), f32),
            *[pltpu.VMEM((2, tiles, ROWS, LANES), f32)] * 2,
            *[pltpu.VMEM((2, groups, ROWS, LANES), jnp.int32)] * 2,
            *[pltpu.VMEM((2, ROWS, LANES), f32)] * 2,
            pltpu.SemaphoreType.DMA((6,)),
            pltpu.SemaphoreType.DMA((COLOURS, 4)),
            pltpu.SemaphoreType.DMA((COLOURS, 4)),
            pltpu.SemaphoreType.DMA((2, 3)),
            pltpu.SemaphoreType.DMA((2, 3)),
        ],
        compiler_params=pltpu.CompilerParams(
            collective_id=0, has_side_effects=True, vmem_limit_bytes=16 * 2**20),
    )(*[pltpu.with_memory_space_constraint(x, pltpu.HBM) for x in arrays])
    return both[0], both[1]


def solution(mesh):
    both = ("dom", "sub")
    placed = (
        P(None, both),
        P(None, None, both),
        P(None, None, both),
        P(None, None, None, both),
        P(None, both),
        P(both),
        P(None, None, both),
    )
    return jax.shard_map(
        functools.partial(shards, mesh.shape["dom"], mesh.shape["sub"]),
        mesh=mesh,
        in_specs=placed,
        out_specs=(P(None, both), P(None, both)),
        check_vma=False,
    )
```
